32 devices in a mesh: dp: 8 (over y, x, core), tensor: 4 (over z).
Axes of the slice: x: 2, y: 2, z: 4, core: 2. Of those that a mesh axis runs over, the one named last changes fastest.
Arguments:
- tokens: bfloat16 [2048, 4096], P('dp', 'tensor'), may hold values from -6 to 6
- weights: bfloat16 [512, 16, 4, 256], P(None, 'tensor'), may hold values from -0.25 to 0.25
- upstream: bfloat16 [2048, 4096], P('dp', 'tensor'), may hold values from -6 to 6
Outputs:
- activated: bfloat16 [2048, 4096], P('dp', 'tensor')
- token_grad: bfloat16 [2048, 4096], P('dp', 'tensor')
- weight_grad: float32 [512, 16, 4, 256], P('dp', 'tensor')
The draws below stay inside these ranges and needn't reach their ends.
All inputs are finite; a program needn't handle non-finite values.
Results may differ from the reference program's by a relative error of at most 0.018.
Values may be sent and summed in bfloat16 or wider, within the bound.
A program may use at most 64 MiB of HBM per device.

```python
import math
import jax
import jax.numpy as jnp

D = 4096
BLOCK_FEATURES = 256
FACTORS = 4
NB = 16
TOKENS = 2048


def block_levels(key, shape, cuts, smallest, top_value):
    loudness = 1.0
    for axis_at, shards_of in cuts:
        steps = jax.random.uniform(jax.random.fold_in(jax.random.fold_in(key, 6), axis_at), (shards_of,), jnp.float32, smallest / len(cuts), top_value / len(cuts))
        loudness = loudness * jnp.repeat(jnp.exp(steps), shape[axis_at] // shards_of).reshape((-1,) + (1,) * (len(shape) - 1 - axis_at))
    return loudness


def scatter_about(stream_key, shape, deviation, most, cuts=(), dtype=jnp.bfloat16):
    result = jax.random.normal(stream_key, shape, jnp.float32) * deviation
    if len(cuts) > 0:
        result = block_levels(stream_key, shape, cuts, -0.22, 0.18) * result
    return jnp.clip(result, min=-most, max=most).astype(dtype)


def setup_inputs(seed: int = 0) -> dict:
    splits = jax.random.split(jax.random.key(seed), 4)
    return {
        "tokens": scatter_about(splits[0], (TOKENS, D), 1.0, 6.0, ((0, 8), (1, 4))),
        "weights": scatter_about(splits[1], (2 * BLOCK_FEATURES, NB, FACTORS, BLOCK_FEATURES), (2 * BLOCK_FEATURES) ** -0.5, 0.25, ((1, 4),)),
        "upstream": scatter_about(splits[2], (TOKENS, D), 1.0, 6.0, ((0, 8), (1, 4))),
    }


def partner_of(values, distance):
    count, blocks, width = values.shape
    folded = values.reshape(count, blocks // (2 * distance), 2, distance, width)
    return folded[:, :, ::-1].reshape(count, blocks, width)

def reference(tokens, weights, upstream):
    layer_number = tokens.reshape(TOKENS, NB, BLOCK_FEATURES)
    gathered_inputs_list = []
    for factor_matrix in range(FACTORS):
        partner = partner_of(layer_number, 2 ** factor_matrix)
        gathered_input = jnp.concatenate([layer_number, partner], axis=2)
        gathered_inputs_list.append(gathered_input)
        layer_number = jnp.einsum('hjk,kjg->hjg', gathered_input.astype(jnp.float32), weights[:, :, factor_matrix, :].astype(jnp.float32)).astype(jnp.bfloat16)
    last = layer_number.astype(jnp.float32)
    activated = jax.nn.gelu(last).astype(jnp.bfloat16).reshape(TOKENS, D)
    _, pull = jax.vjp(jax.nn.gelu, last)
    current_gradient = pull(upstream.reshape(TOKENS, NB, BLOCK_FEATURES).astype(jnp.float32))[0].astype(jnp.bfloat16)
    scale_factor = 1.0 / math.sqrt(TOKENS)
    gradient_collection = [None] * FACTORS
    for factor_matrix in reversed(range(FACTORS)):
        factor_weight = weights[:, :, factor_matrix, :].astype(jnp.float32)
        factor_gradient = current_gradient.astype(jnp.float32)
        gradient_collection[factor_matrix] = scale_factor * jnp.einsum('urs,urd->srd', gathered_inputs_list[factor_matrix].astype(jnp.float32), factor_gradient)
        passed_input = jnp.einsum('jvu,rvu->jvr', factor_gradient, factor_weight[BLOCK_FEATURES:]).astype(jnp.bfloat16)
        self_portion = jnp.einsum('jvu,rvu->jvr', factor_gradient, factor_weight[:BLOCK_FEATURES])
        current_gradient = (self_portion + partner_of(passed_input, 2 ** factor_matrix).astype(jnp.float32)).astype(jnp.bfloat16)
    token_grad = current_gradient.reshape(TOKENS, D)
    weight_grad = jnp.stack(gradient_collection, axis=2)
    return (activated, token_grad, weight_grad)
```

```python
import functools
import math

import jax
import jax.numpy as jnp
from jax import lax
from jax.experimental import pallas as pl
from jax.experimental.pallas import tpu as pltpu
from jax.sharding import PartitionSpec as P

BLOCK_FEATURES = 256
FACTORS = 4


def partner_2(block, axis, stride):
    count = lax.axis_size(axis)
    route = []
    for low in range(count):
        high = low | 1 << stride
        if high != low and high < count:
            route += [(low, high), (high, low)]
    return lax.ppermute(block, axis, route)


def local_partner(values, distance):
    count, blocks, width = values.shape
    folded = values.reshape(count, blocks // (2 * distance), 2, distance, width)
    return folded[:, :, ::-1].reshape(count, blocks, width)


def level_of(distance, blocks):
    return (distance // blocks).bit_length() - 1


def forward_partner(values, distance):
    blocks = values.shape[1]
    if distance < blocks:
        return local_partner(values, distance)
    return partner_2(values, "tensor", level_of(distance, blocks))


def backward_partner(values, distance):
    blocks = values.shape[1]
    if distance < blocks:
        return local_partner(values, distance)
    return partner_2(values, "tensor", level_of(distance, blocks))


def again_partner(values, distance):
    blocks = values.shape[1]
    if distance < blocks:
        return local_partner(values, distance)
    return partner_2(values, "tensor", level_of(distance, blocks))


def grad_block(gathered_input, following_gradient, scale_factor):
    return scale_factor * jnp.einsum(
        "urs,urd->srd", gathered_input, following_gradient, preferred_element_type=jnp.float32
    )


def plain_device(tokens, weights, upstream):
    tok_count = tokens.shape[0]
    blocks = tokens.shape[1] // BLOCK_FEATURES
    scale_factor = 1.0 / math.sqrt(tok_count * lax.axis_size("dp"))
    layer_number = tokens.reshape(tok_count, blocks, BLOCK_FEATURES)
    inputs_saved = []
    partners_saved = []
    for factor_matrix in range(FACTORS):
        partner = forward_partner(layer_number, 2**factor_matrix)
        inputs_saved.append(layer_number)
        partners_saved.append(partner)
        gathered_input = jnp.concatenate([layer_number, partner], axis=2)
        layer_number = jnp.einsum(
            "hjk,kjg->hjg",
            gathered_input,
            weights[:, :, factor_matrix, :],
            preferred_element_type=jnp.float32,
        ).astype(jnp.bfloat16)
    last = layer_number.astype(jnp.float32)
    activated = jax.nn.gelu(last).astype(jnp.bfloat16).reshape(tok_count, blocks * BLOCK_FEATURES)
    _, pull = jax.vjp(jax.nn.gelu, last)
    current_gradient = pull(
        upstream.reshape(tok_count, blocks, BLOCK_FEATURES).astype(jnp.float32)
    )[0].astype(jnp.bfloat16)
    joined_all = [None] * FACTORS
    grads_next = [None] * FACTORS
    for factor_matrix in reversed(range(FACTORS)):
        distance = 2**factor_matrix
        factor_weight = weights[:, :, factor_matrix, :]
        partner = again_partner(inputs_saved[factor_matrix], distance)
        gathered_input = jnp.concatenate([inputs_saved[factor_matrix], partner], axis=2)
        joined_all[factor_matrix] = gathered_input
        grads_next[factor_matrix] = current_gradient
        passed_input = jnp.einsum(
            "jvu,rvu->jvr",
            current_gradient,
            factor_weight[BLOCK_FEATURES:],
            preferred_element_type=jnp.float32,
        ).astype(jnp.bfloat16)
        self_portion = jnp.einsum(
            "jvu,rvu->jvr",
            current_gradient,
            factor_weight[:BLOCK_FEATURES],
            preferred_element_type=jnp.float32,
        )
        arrived = backward_partner(passed_input, distance)
        current_gradient = (self_portion + arrived.astype(jnp.float32)).astype(jnp.bfloat16)
    pieces = [
        grad_block(joined_all[factor_matrix], grads_next[factor_matrix], scale_factor)
        for factor_matrix in range(FACTORS)
    ]
    weight_grad = lax.psum_scatter(jnp.stack(pieces, axis=2), "dp", scatter_dimension=0, tiled=True)
    token_grad = current_gradient.reshape(tok_count, blocks * BLOCK_FEATURES)
    return (activated, token_grad, weight_grad)


CHUNKS = 4
MESH = pl.DeviceIdType.MESH
W = BLOCK_FEATURES
NN = (((1,), (0,)), ((), ()))
NT = (((1,), (1,)), ((), ()))
TN = (((0,), (0,)), ((), ()))
GELU_A = 0.7978845608
GELU_B = 0.044715


def dot(a, b, dims):
    return lax.dot_general(a, b, dims, preferred_element_type=jnp.float32)


def flip(index, bit):
    return index + bit - 2 * bit * (lax.rem(index // bit, 2))


def fused_kernel(
    scale_factor,
    tok_ref,
    up_ref,
    w_hbm,
    act_out,
    tg_out,
    wg_out,
    w,
    z,
    part,
    grad,
    hand,
    hand_in,
    self_part,
    act,
    tgrad,
    wg,
    wg_core,
    wg_sum,
    wg_in,
    wg_fin,
    w_sem,
    out_sem,
    z_send,
    z_recv,
    core_send,
    core_recv,
    chip_send,
    chip_recv,
):
    rows = tok_ref.shape[0]
    blocks = tok_ref.shape[1] // W
    step = rows // CHUNKS
    shard = wg_fin.shape[2]
    dp = lax.axis_index("dp")
    tensor = lax.axis_index("tensor")
    core = lax.rem(dp, 2)
    chip = dp // 2

    loads = []
    for k in range(FACTORS):
        load = pltpu.make_async_copy(w_hbm.at[k], w.at[k], w_sem.at[k])
        load.start()
        loads.append(load)

    near = (dp, flip(tensor, 1))
    far = (dp, flip(tensor, 2))
    sibling = (flip(dp, 1), tensor)
    chips = [flip(chip, 1), flip(chip, 2), 3 - chip]
    others = [(2 * c + core, tensor) for c in chips]

    barrier = pltpu.get_barrier_semaphore()
    for device in [near, far, sibling] + others:
        pl.semaphore_signal(barrier, inc=1, device_id=device, device_id_type=MESH)
    pl.semaphore_wait(barrier, 6)

    def span(c):
        return slice(c * step, (c + 1) * step)

    def col(i):
        return slice(i * W, (i + 1) * W)

    def z_copy(stage, c):
        src = (z.at[2], z.at[3], hand.at[1], hand.at[0])[stage]
        dst = (part.at[0], part.at[1], hand_in.at[1], hand_in.at[0])[stage]
        return pltpu.make_async_remote_copy(
            src_ref=src.at[pl.ds(c * step, step)],
            dst_ref=dst.at[pl.ds(c * step, step)],
            send_sem=z_send.at[stage, c],
            recv_sem=z_recv.at[stage, c],
            device_id=(near, far, far, near)[stage],
            device_id_type=MESH,
        )

    def z_value(k, c, i):
        if k == 0:
            return tok_ref[span(c), col(i)]
        return z[k, span(c), col(i)]

    def partner_value(k, c, i):
        if k < 2:
            return z_value(k, c, i ^ (1 << k))
        return part[k - 2, span(c), col(i)]

    def factor(k, c, i):
        return dot(z_value(k, c, i), w[k, i, :W, :], NN) + dot(
            partner_value(k, c, i), w[k, i, W:, :], NN
        )

    def stage_f1(c):
        for k in range(2):
            if c == 0:
                loads[k].wait()
            for i in range(blocks):
                z[k + 1, span(c), col(i)] = factor(k, c, i).astype(jnp.bfloat16)
        z_copy(0, c).start()

    def stage_f2(c):
        if c == 0:
            loads[2].wait()
        z_copy(0, c).wait_recv()
        for i in range(blocks):
            z[3, span(c), col(i)] = factor(2, c, i).astype(jnp.bfloat16)
        z_copy(1, c).start()

    def stage_f3(c):
        if c == 0:
            loads[3].wait()
        z_copy(1, c).wait_recv()
        for i in range(blocks):
            v = factor(3, c, i).astype(jnp.bfloat16).astype(jnp.float32)
            square = v * v
            t = jnp.tanh(GELU_A * (v + GELU_B * (v * square)))
            half = 0.5 * (1.0 + t)
            act[span(c), col(i)] = (v * half).astype(jnp.bfloat16)
            slope = half + (0.5 * v) * (1.0 - t * t) * (GELU_A * (1.0 + 3.0 * GELU_B * square))
            g = (up_ref[span(c), col(i)].astype(jnp.float32) * slope).astype(jnp.bfloat16)
            grad[3, span(c), col(i)] = g
            hand[1, span(c), col(i)] = dot(g, w[3, i, W:, :], NT).astype(jnp.bfloat16)
        z_copy(2, c).start()
        for i in range(blocks):
            self_part[1, span(c), col(i)] = dot(grad[3, span(c), col(i)], w[3, i, :W, :], NT)

    def stage_b3(c):
        z_copy(2, c).wait_recv()
        for i in range(blocks):
            g = self_part[1, span(c), col(i)] + hand_in[1, span(c), col(i)].astype(jnp.float32)
            g = g.astype(jnp.bfloat16)
            grad[2, span(c), col(i)] = g
            hand[0, span(c), col(i)] = dot(g, w[2, i, W:, :], NT).astype(jnp.bfloat16)
        z_copy(3, c).start()
        for i in range(blocks):
            self_part[0, span(c), col(i)] = dot(grad[2, span(c), col(i)], w[2, i, :W, :], NT)

    def stage_b2(c):
        z_copy(3, c).wait_recv()
        for i in range(blocks):
            g = self_part[0, span(c), col(i)] + hand_in[0, span(c), col(i)].astype(jnp.float32)
            grad[1, span(c), col(i)] = g.astype(jnp.bfloat16)
        for k in (1, 0):
            both = [dot(grad[k, span(c), col(i)], w[k, i], NT) for i in range(blocks)]
            for i in range(blocks):
                handed = both[i ^ (1 << k)][:, W:].astype(jnp.bfloat16).astype(jnp.float32)
                g = (both[i][:, :W] + handed).astype(jnp.bfloat16)
                if k == 1:
                    grad[0, span(c), col(i)] = g
                else:
                    tgrad[span(c), col(i)] = g

    def core_copy(k):
        return pltpu.make_async_remote_copy(
            src_ref=wg.at[k, 1 - core],
            dst_ref=wg_core.at[k],
            send_sem=core_send.at[k],
            recv_sem=core_recv.at[k],
            device_id=sibling,
            device_id_type=MESH,
        )

    def chip_copy(k, m):
        return pltpu.make_async_remote_copy(
            src_ref=wg_sum.at[k, chips[m]],
            dst_ref=wg_in.at[k, m],
            send_sem=chip_send.at[k, m],
            recv_sem=chip_recv.at[k, m],
            device_id=others[m],
            device_id_type=MESH,
        )

    def weight_terms(k):
        per = W // shard
        for i in range(blocks):
            g = grad[k, :, col(i)]
            if k == 0:
                lefts = (tok_ref[:, col(i)], tok_ref[:, col(i ^ 1)])
            elif k == 1:
                lefts = (z[1, :, col(i)], z[1, :, col(i ^ 2)])
            else:
                lefts = (z[k, :, col(i)], part[k - 2, :, col(i)])
            for side in range(2):
                total = dot(lefts[side], g, TN).astype(jnp.bfloat16)
                for j in range(per):
                    at = side * per + j
                    wg[k, at % 2, at // 2, i] = total[j * shard : (j + 1) * shard]
        core_copy(k).start()

    def weight_sum(k):
        core_copy(k).wait_recv()
        for c in range(4):
            wg_sum[k, c] = (
                wg[k, core, c].astype(jnp.float32) + wg_core[k, c].astype(jnp.float32)
            ).astype(jnp.bfloat16)
        for m in (2, 0, 1):
            chip_copy(k, m).start()

    def weight_final(k):
        total = wg_sum[k, chip].astype(jnp.float32)
        for m in range(3):
            chip_copy(k, m).wait_recv()
            total = total + wg_in[k, m].astype(jnp.float32)
        wg_fin[k] = total * scale_factor
        copy = pltpu.make_async_copy(wg_fin.at[k], wg_out.at[k], out_sem.at[2 + k])
        copy.start()
        return copy

    last = CHUNKS - 1
    work = []
    skew = 2
    for stage, run in enumerate((stage_f1, stage_f2, stage_f3, stage_b3, stage_b2)):
        for c in range(CHUNKS):
            work.append((c + skew * stage, -stage, functools.partial(run, c)))
    outs = []

    def store_act():
        outs.append(pltpu.make_async_copy(act, act_out, out_sem.at[0]))
        outs[-1].start()

    def store_tgrad():
        outs.append(pltpu.make_async_copy(tgrad, tg_out, out_sem.at[1]))
        outs[-1].start()

    work.append((last + skew * 2, 1, store_act))
    work.append((last + skew * 2, 2, lambda: weight_terms(3)))
    work.append((last + skew * 2 + 1, 1, lambda: weight_sum(3)))
    work.append((last + skew * 3, 1, lambda: weight_terms(2)))
    work.append((last + skew * 3 + 1, 1, lambda: weight_sum(2)))
    for _, _, run in sorted(work, key=lambda item: item[:2]):
        run()
    weight_terms(1)
    weight_terms(0)
    store_tgrad()
    weight_sum(1)
    weight_sum(0)
    for k in (3, 2, 1, 0):
        outs.append(weight_final(k))
    for stage in range(4):
        for c in range(CHUNKS):
            z_copy(stage, c).wait_send()
    for k in range(FACTORS):
        core_copy(k).wait_send()
        for m in range(3):
            chip_copy(k, m).wait_send()
    for copy in outs:
        copy.wait()


def fused_device(tokens, weights, upstream):
    rows, width = tokens.shape
    blocks = width // W
    dp = lax.axis_size("dp")
    shard = 2 * W // dp
    scale_factor = 1.0 / math.sqrt(rows * dp)
    w = weights.transpose(2, 1, 0, 3)
    bf16, f32 = jnp.bfloat16, jnp.float32
    dma = pltpu.SemaphoreType.DMA
    whole = pltpu.VMEM((rows, width), bf16)
    activated, token_grad, weight_grad = pl.pallas_call(
        functools.partial(fused_kernel, scale_factor),
        out_shape=(
            jax.ShapeDtypeStruct((rows, width), bf16),
            jax.ShapeDtypeStruct((rows, width), bf16),
            jax.ShapeDtypeStruct((FACTORS, blocks, shard, W), f32),
        ),
        in_specs=[
            pl.BlockSpec(memory_space=pltpu.VMEM),
            pl.BlockSpec(memory_space=pltpu.VMEM),
            pl.BlockSpec(memory_space=pl.ANY),
        ],
        out_specs=[pl.BlockSpec(memory_space=pl.ANY)] * 3,
        scratch_shapes=[
            pltpu.VMEM((FACTORS, blocks, 2 * W, W), bf16),
            pltpu.VMEM((4, rows, width), bf16),
            pltpu.VMEM((2, rows, width), bf16),
            pltpu.VMEM((4, rows, width), bf16),
            pltpu.VMEM((2, rows, width), bf16),
            pltpu.VMEM((2, rows, width), bf16),
            pltpu.VMEM((2, rows, width), f32),
            whole,
            whole,
            pltpu.VMEM((FACTORS, 2, 4, blocks, shard, W), bf16),
            pltpu.VMEM((FACTORS, 4, blocks, shard, W), bf16),
            pltpu.VMEM((FACTORS, 4, blocks, shard, W), bf16),
            pltpu.VMEM((FACTORS, 3, blocks, shard, W), bf16),
            pltpu.VMEM((FACTORS, blocks, shard, W), f32),
            dma((FACTORS,)),
            dma((2 + FACTORS,)),
            dma((4, CHUNKS)),
            dma((4, CHUNKS)),
            dma((FACTORS,)),
            dma((FACTORS,)),
            dma((FACTORS, 3)),
            dma((FACTORS, 3)),
        ],
        compiler_params=pltpu.CompilerParams(
            collective_id=0, has_side_effects=True, vmem_limit_bytes=48 * 1024 * 1024
        ),
        name="butterfly",
    )(tokens, upstream, w)
    return activated, token_grad, weight_grad.transpose(2, 1, 0, 3)


def on_device(tokens, weights, upstream):
    blocks = tokens.shape[1] // BLOCK_FEATURES
    fits = (
        lax.axis_size("dp") == 8
        and lax.axis_size("tensor") == 4
        and blocks == 4
        and tokens.shape[0] % (16 * CHUNKS) == 0
        and tokens.shape[0] <= 256
    )
    if fits:
        return fused_device(tokens, weights, upstream)
    return plain_device(tokens, weights, upstream)


def solution(mesh):
    placed = (P("dp", "tensor"), P(None, "tensor", None, None), P("dp", "tensor"))
    return jax.shard_map(
        on_device,
        mesh=mesh,
        in_specs=placed,
        out_specs=(P("dp", "tensor"), P("dp", "tensor"), P("dp", "tensor", None, None)),
        check_vma=False,
    )
```

```python
import functools
import math

import jax
import jax.numpy as jnp
from jax import lax
from jax.experimental import pallas as pl
from jax.experimental.pallas import tpu as pltpu
from jax.sharding import PartitionSpec as P

BLOCK_FEATURES = 256
FACTORS = 4


def partner_2(block, axis, stride):
    count = lax.axis_size(axis)
    route = []
    for low in range(count):
        high = low | 1 << stride
        if high != low and high < count:
            route += [(low, high), (high, low)]
    return lax.ppermute(block, axis, route)


def local_partner(values, distance):
    count, blocks, width = values.shape
    folded = values.reshape(count, blocks // (2 * distance), 2, distance, width)
    return folded[:, :, ::-1].reshape(count, blocks, width)


def level_of(distance, blocks):
    return (distance // blocks).bit_length() - 1


def forward_partner(values, distance):
    blocks = values.shape[1]
    if distance < blocks:
        return local_partner(values, distance)
    return partner_2(values, "tensor", level_of(distance, blocks))


def backward_partner(values, distance):
    blocks = values.shape[1]
    if distance < blocks:
        return local_partner(values, distance)
    return partner_2(values, "tensor", level_of(distance, blocks))


def again_partner(values, distance):
    blocks = values.shape[1]
    if distance < blocks:
        return local_partner(values, distance)
    return partner_2(values, "tensor", level_of(distance, blocks))


def grad_block(gathered_input, following_gradient, scale_factor):
    return scale_factor * jnp.einsum(
        "urs,urd->srd", gathered_input, following_gradient, preferred_element_type=jnp.float32
    )


def plain_device(tokens, weights, upstream):
    tok_count = tokens.shape[0]
    blocks = tokens.shape[1] // BLOCK_FEATURES
    scale_factor = 1.0 / math.sqrt(tok_count * lax.axis_size("dp"))
    layer_number = tokens.reshape(tok_count, blocks, BLOCK_FEATURES)
    inputs_saved = []
    partners_saved = []
    for factor_matrix in range(FACTORS):
        partner = forward_partner(layer_number, 2**factor_matrix)
        inputs_saved.append(layer_number)
        partners_saved.append(partner)
        gathered_input = jnp.concatenate([layer_number, partner], axis=2)
        layer_number = jnp.einsum(
            "hjk,kjg->hjg",
            gathered_input,
            weights[:, :, factor_matrix, :],
            preferred_element_type=jnp.float32,
        ).astype(jnp.bfloat16)
    last = layer_number.astype(jnp.float32)
    activated = jax.nn.gelu(last).astype(jnp.bfloat16).reshape(tok_count, blocks * BLOCK_FEATURES)
    _, pull = jax.vjp(jax.nn.gelu, last)
    current_gradient = pull(
        upstream.reshape(tok_count, blocks, BLOCK_FEATURES).astype(jnp.float32)
    )[0].astype(jnp.bfloat16)
    joined_all = [None] * FACTORS
    grads_next = [None] * FACTORS
    for factor_matrix in reversed(range(FACTORS)):
        distance = 2**factor_matrix
        factor_weight = weights[:, :, factor_matrix, :]
        partner = again_partner(inputs_saved[factor_matrix], distance)
        gathered_input = jnp.concatenate([inputs_saved[factor_matrix], partner], axis=2)
        joined_all[factor_matrix] = gathered_input
        grads_next[factor_matrix] = current_gradient
        passed_input = jnp.einsum(
            "jvu,rvu->jvr",
            current_gradient,
            factor_weight[BLOCK_FEATURES:],
            preferred_element_type=jnp.float32,
        ).astype(jnp.bfloat16)
        self_portion = jnp.einsum(
            "jvu,rvu->jvr",
            current_gradient,
            factor_weight[:BLOCK_FEATURES],
            preferred_element_type=jnp.float32,
        )
        arrived = backward_partner(passed_input, distance)
        current_gradient = (self_portion + arrived.astype(jnp.float32)).astype(jnp.bfloat16)
    pieces = [
        grad_block(joined_all[factor_matrix], grads_next[factor_matrix], scale_factor)
        for factor_matrix in range(FACTORS)
    ]
    weight_grad = lax.psum_scatter(jnp.stack(pieces, axis=2), "dp", scatter_dimension=0, tiled=True)
    token_grad = current_gradient.reshape(tok_count, blocks * BLOCK_FEATURES)
    return (activated, token_grad, weight_grad)


SKEW = 1
REDO = (3,)
ORDER = (0, 2, 1, 3)
MESH = pl.DeviceIdType.MESH
W = BLOCK_FEATURES
NN = (((1,), (0,)), ((), ()))
NT = (((1,), (1,)), ((), ()))
TN = (((0,), (0,)), ((), ()))
GELU_A = 0.7978845608
GELU_B = 0.044715


def dot(a, b, dims):
    return lax.dot_general(a, b, dims, preferred_element_type=jnp.float32)


def flip(index, bit):
    return index + bit - 2 * bit * (lax.rem(index // bit, 2))


def fused_kernel(
    scale_factor,
    tok_ref,
    up_ref,
    w_hbm,
    act_out,
    tg_out,
    wg_out,
    w,
    w_far,
    up_far,
    z,
    part,
    grad,
    hand,
    hand_in,
    self_part,
    act,
    tgrad,
    wg,
    wg_core,
    wg_sum,
    wg_in,
    wg_fin,
    w_sem,
    out_sem,
    z_send,
    z_recv,
    core_send,
    core_recv,
    chip_send,
    chip_recv,
    far_send,
    far_recv,
    share_send,
    share_recv,
):
    rows = tok_ref.shape[0]
    blocks = tok_ref.shape[1] // W
    shard = wg_fin.shape[2]
    dp = lax.axis_index("dp")
    tensor = lax.axis_index("tensor")
    core = lax.rem(dp, 2)
    chip = dp // 2

    loads = []
    for k in range(FACTORS):
        load = pltpu.make_async_copy(w_hbm.at[k], w.at[k], w_sem.at[k])
        load.start()
        loads.append(load)

    near = (dp, flip(tensor, 1))
    far = (dp, flip(tensor, 2))
    sibling = (flip(dp, 1), tensor)
    chips = [flip(chip, 1), flip(chip, 2), 3 - chip]
    others = [(2 * c + core, tensor) for c in chips]

    barrier = pltpu.get_barrier_semaphore()
    peers = [dp]
    for bit in (1, 2, 4):
        peers += [flip(p, bit) for p in peers]
    for device in [near, far] + [(p, tensor) for p in peers[1:]]:
        pl.semaphore_signal(barrier, inc=1, device_id=device, device_id_type=MESH)
    pl.semaphore_wait(barrier, 9)
    mine = pl.ds(pl.multiple_of(dp * shard, shard), shard)

    def far_copy(r, what):
        i = REDO[r]
        src = up_ref.at[:, i * W : (i + 1) * W] if what else w_hbm.at[3, i, mine]
        return pltpu.make_async_remote_copy(
            src_ref=src,
            dst_ref=up_far.at[r] if what else w_far.at[r, mine],
            send_sem=far_send.at[r, what],
            recv_sem=far_recv.at[r, what],
            device_id=far,
            device_id_type=MESH,
        )

    def share_copy(r, m, sender=None):
        rows_of = pl.ds(pl.multiple_of((dp if sender is None else sender) * shard, shard), shard)
        return pltpu.make_async_remote_copy(
            src_ref=w_far.at[r, rows_of],
            dst_ref=w_far.at[r, rows_of],
            send_sem=share_send.at[r, m - 1],
            recv_sem=share_recv.at[r, m - 1],
            device_id=(peers[m], tensor),
            device_id_type=MESH,
        )

    for what in (0, 1):
        for r in range(len(REDO)):
            far_copy(r, what).start()

    def col(i):
        return slice(i * W, (i + 1) * W)

    def z_copy(stage, i):
        src = (z.at[2], z.at[3], hand.at[1], hand.at[0])[stage]
        dst = (part.at[0], part.at[1], hand_in.at[1], hand_in.at[0])[stage]
        return pltpu.make_async_remote_copy(
            src_ref=src.at[i],
            dst_ref=dst.at[i],
            send_sem=z_send.at[stage, i],
            recv_sem=z_recv.at[stage, i],
            device_id=(near, far, far, near)[stage],
            device_id_type=MESH,
        )

    def z_value(k, i):
        return tok_ref[:, col(i)] if k == 0 else z[k, i]

    def partner_value(k, i):
        return z_value(k, i ^ (1 << k)) if k < 2 else part[k - 2, i]

    def factor(k, i):
        total = dot(z_value(k, i), w[k, i, :W, :], NN)
        return (total + dot(partner_value(k, i), w[k, i, W:, :], NN)).astype(jnp.bfloat16)

    def stage_f1(i):
        z[2, i] = factor(1, i)
        z_copy(0, i).start()

    def stage_f2(i):
        z_copy(0, i).wait_recv()
        z[3, i] = factor(2, i)
        z_copy(1, i).start()

    def gelu_slope(v):
        square = v * v
        t = jnp.tanh(GELU_A * (v + GELU_B * (v * square)))
        half = 0.5 * (1.0 + t)
        slope = half + (0.5 * v) * (1.0 - t * t) * (GELU_A * (1.0 + 3.0 * GELU_B * square))
        return half, slope

    def stage_f3(i):
        z_copy(1, i).wait_recv()
        v = factor(3, i).astype(jnp.float32)
        half, slope = gelu_slope(v)
        act[:, col(i)] = (v * half).astype(jnp.bfloat16)
        g = (up_ref[:, col(i)].astype(jnp.float32) * slope).astype(jnp.bfloat16)
        grad[3, i] = g
        if i in REDO:
            r = REDO.index(i)
            for m in range(1, len(peers)):
                share_copy(r, m, peers[m]).wait_recv()
            far_copy(r, 1).wait_recv()
            v = dot(part[1, i], w_far[r, :W, :], NN) + dot(z[3, i], w_far[r, W:, :], NN)
            _, slope = gelu_slope(v.astype(jnp.bfloat16).astype(jnp.float32))
            g = (up_far[r].astype(jnp.float32) * slope).astype(jnp.bfloat16)
            hand_in[1, i] = dot(g, w_far[r, W:, :], NT).astype(jnp.bfloat16)
        else:
            hand[1, i] = dot(g, w[3, i, W:, :], NT).astype(jnp.bfloat16)
            z_copy(2, i).start()
        self_part[1, i] = dot(grad[3, i], w[3, i, :W, :], NT)
        if i in REDO:
            stage_b3(i)
        weight_terms(3, i)

    def stage_b3(i):
        if i not in REDO:
            z_copy(2, i).wait_recv()
        g = (self_part[1, i] + hand_in[1, i].astype(jnp.float32)).astype(jnp.bfloat16)
        grad[2, i] = g
        hand[0, i] = dot(g, w[2, i, W:, :], NT).astype(jnp.bfloat16)
        z_copy(3, i).start()
        self_part[0, i] = dot(grad[2, i], w[2, i, :W, :], NT)
        weight_terms(2, i)

    def stage_b2(i):
        z_copy(3, i).wait_recv()
        g = self_part[0, i] + hand_in[0, i].astype(jnp.float32)
        grad[1, i] = g.astype(jnp.bfloat16)
        weight_terms(1, i)

    def stage_local(k, i, j):
        both = {m: dot(grad[k, m], w[k, m], NT) for m in (i, j)}
        for m, n in ((i, j), (j, i)):
            handed = both[n][:, W:].astype(jnp.bfloat16).astype(jnp.float32)
            g = (both[m][:, :W] + handed).astype(jnp.bfloat16)
            if k == 1:
                grad[0, m] = g
            else:
                tgrad[:, col(m)] = g

    def core_copy(k, i):
        return pltpu.make_async_remote_copy(
            src_ref=wg.at[k, i, 1 - core],
            dst_ref=wg_core.at[k, i],
            send_sem=core_send.at[k, i],
            recv_sem=core_recv.at[k, i],
            device_id=sibling,
            device_id_type=MESH,
        )

    def chip_copy(k, i, m):
        return pltpu.make_async_remote_copy(
            src_ref=wg_sum.at[k, i, chips[m]],
            dst_ref=wg_in.at[k, i, m],
            send_sem=chip_send.at[k, i, m],
            recv_sem=chip_recv.at[k, i, m],
            device_id=others[m],
            device_id_type=MESH,
        )

    def weight_terms(k, i):
        per = W // shard
        g = grad[k, i]
        for side, left in enumerate((z_value(k, i), partner_value(k, i))):
            total = dot(left, g, TN).astype(jnp.bfloat16)
            for j in range(per):
                at = side * per + j
                wg[k, i, at % 2, at // 2] = total[j * shard : (j + 1) * shard]
        core_copy(k, i).start()

    def weight_sum(k, i):
        core_copy(k, i).wait_recv()
        kept = wg[k, i, core].astype(jnp.float32)
        wg_sum[k, i] = (kept + wg_core[k, i].astype(jnp.float32)).astype(jnp.bfloat16)
        for m in (2, 0, 1):
            chip_copy(k, i, m).start()

    def weight_final(k, i):
        total = wg_sum[k, i, chip].astype(jnp.float32)
        for m in range(3):
            chip_copy(k, i, m).wait_recv()
            total = total + wg_in[k, i, m].astype(jnp.float32)
        wg_fin[k, i] = total * scale_factor

    outs = []

    def store(src, dst, slot):
        outs.append(pltpu.make_async_copy(src, dst, out_sem.at[slot]))
        outs[-1].start()

    loads[0].wait()
    for i in range(blocks):
        z[1, i] = factor(0, i)
    for load in loads[1:]:
        load.wait()

    order = ORDER
    work = []
    for p, i in enumerate(order):
        for stage, run in enumerate((stage_f1, stage_f2, stage_f3, stage_b3, stage_b2)):
            if i in REDO and run is stage_b3:
                continue
            work.append((p + SKEW * stage, -stage, functools.partial(run, i)))
        for k, stage in ((3, 2), (2, 3)):
            work.append((p + SKEW * stage + 1, 1, functools.partial(weight_sum, k, i)))
    def share():
        for r in range(len(REDO)):
            far_copy(r, 0).wait_recv()
            for m in (6, 7, 2, 3, 4, 5, 1):
                share_copy(r, m).start()

    work.append((1, 1, functools.partial(share)))
    for _, _, run in sorted(work, key=lambda item: item[:2]):
        if run.func is stage_b2 and run.args[0] == 1:
            store(act, act_out, 0)
            stage_local(1, 0, 2)
            weight_terms(0, 0)
            weight_terms(0, 2)
            weight_sum(1, 0)
            weight_sum(1, 2)
        run()
        if run.func is stage_b2 and run.args[0] == 1:
            weight_sum(0, 0)
            weight_sum(0, 2)
    stage_local(1, 1, 3)
    weight_terms(0, 1)
    weight_terms(0, 3)
    for k, i in ((1, 1), (1, 3), (0, 1), (0, 3)):
        weight_sum(k, i)
    stage_local(0, 0, 1)
    stage_local(0, 2, 3)
    store(tgrad, tg_out, 1)
    for k in (3, 2, 1, 0):
        for i in order:
            weight_final(k, i)
        store(wg_fin.at[k], wg_out.at[k], 2 + k)
    for i in range(blocks):
        for stage in range(4):
            if stage != 2 or i not in REDO:
                z_copy(stage, i).wait_send()
        for k in range(FACTORS):
            core_copy(k, i).wait_send()
            for m in range(3):
                chip_copy(k, i, m).wait_send()
    for r in range(len(REDO)):
        for what in (0, 1):
            far_copy(r, what).wait_send()
        for m in range(1, len(peers)):
            share_copy(r, m).wait_send()
    for copy in outs:
        copy.wait()


def finish_kernel(act_ref, tg_ref, wg_ref, act_out, tg_out, wg_out):
    act_out[...] = act_ref[...]
    tg_out[...] = tg_ref[...]
    for k in range(FACTORS):
        for i in range(wg_ref.shape[1]):
            wg_out[:, i, k, :] = wg_ref[k, i]


def fused_device(tokens, weights, upstream):
    rows, width = tokens.shape
    blocks = width // W
    dp = lax.axis_size("dp")
    shard = 2 * W // dp
    scale_factor = 1.0 / math.sqrt(rows * dp)
    w = weights.transpose(2, 1, 0, 3)
    bf16, f32 = jnp.bfloat16, jnp.float32
    dma = pltpu.SemaphoreType.DMA
    whole = pltpu.VMEM((rows, width), bf16)
    activated, token_grad, weight_grad = pl.pallas_call(
        functools.partial(fused_kernel, scale_factor),
        out_shape=(
            jax.ShapeDtypeStruct((rows, width), bf16),
            jax.ShapeDtypeStruct((rows, width), bf16),
            jax.ShapeDtypeStruct((FACTORS, blocks, shard, W), f32),
        ),
        in_specs=[
            pl.BlockSpec(memory_space=pltpu.VMEM),
            pl.BlockSpec(memory_space=pltpu.VMEM),
            pl.BlockSpec(memory_space=pl.ANY),
        ],
        out_specs=[pl.BlockSpec(memory_space=pl.ANY)] * 3,
        scratch_shapes=[
            pltpu.VMEM((FACTORS, blocks, 2 * W, W), bf16),
            pltpu.VMEM((len(REDO), 2 * W, W), bf16),
            pltpu.VMEM((len(REDO), rows, W), bf16),
            pltpu.VMEM((4, blocks, rows, W), bf16),
            pltpu.VMEM((2, blocks, rows, W), bf16),
            pltpu.VMEM((4, blocks, rows, W), bf16),
            pltpu.VMEM((2, blocks, rows, W), bf16),
            pltpu.VMEM((2, blocks, rows, W), bf16),
            pltpu.VMEM((2, blocks, rows, W), f32),
            whole,
            whole,
            pltpu.VMEM((FACTORS, blocks, 2, 4, shard, W), bf16),
            pltpu.VMEM((FACTORS, blocks, 4, shard, W), bf16),
            pltpu.VMEM((FACTORS, blocks, 4, shard, W), bf16),
            pltpu.VMEM((FACTORS, blocks, 3, shard, W), bf16),
            pltpu.VMEM((FACTORS, blocks, shard, W), f32),
            dma((FACTORS,)),
            dma((2 + FACTORS,)),
            dma((4, blocks)),
            dma((4, blocks)),
            dma((FACTORS, blocks)),
            dma((FACTORS, blocks)),
            dma((FACTORS, blocks, 3)),
            dma((FACTORS, blocks, 3)),
            dma((len(REDO), 2)),
            dma((len(REDO), 2)),
            dma((len(REDO), 7)),
            dma((len(REDO), 7)),
        ],
        compiler_params=pltpu.CompilerParams(
            collective_id=0, has_side_effects=True, vmem_limit_bytes=48 * 1024 * 1024
        ),
        name="butterfly",
    )(tokens, upstream, w)
    return pl.pallas_call(
        finish_kernel,
        out_shape=(
            jax.ShapeDtypeStruct((rows, width), bf16),
            jax.ShapeDtypeStruct((rows, width), bf16),
            jax.ShapeDtypeStruct((shard, blocks, FACTORS, W), f32),
        ),
        in_specs=[pl.BlockSpec(memory_space=pltpu.VMEM)] * 3,
        out_specs=[pl.BlockSpec(memory_space=pltpu.VMEM)] * 3,
        compiler_params=pltpu.CompilerParams(vmem_limit_bytes=16 * 1024 * 1024),
        name="finish",
    )(activated, token_grad, weight_grad)


def on_device(tokens, weights, upstream):
    blocks = tokens.shape[1] // BLOCK_FEATURES
    fits = (
        lax.axis_size("dp") == 8
        and lax.axis_size("tensor") == 4
        and blocks == 4
        and tokens.shape[0] % 16 == 0
        and tokens.shape[0] <= 256
    )
    if fits:
        return fused_device(tokens, weights, upstream)
    return plain_device(tokens, weights, upstream)


def solution(mesh):
    placed = (P("dp", "tensor"), P(None, "tensor", None, None), P("dp", "tensor"))
    return jax.shard_map(
        on_device,
        mesh=mesh,
        in_specs=placed,
        out_specs=(P("dp", "tensor"), P("dp", "tensor"), P("dp", "tensor", None, None)),
        check_vma=False,
    )
```

```python
import functools
import math

import jax
import jax.numpy as jnp
from jax import lax
from jax.experimental import pallas as pl
from jax.experimental.pallas import tpu as pltpu
from jax.sharding import PartitionSpec as P

BLOCK_FEATURES = 256
FACTORS = 4


def partner_2(block, axis, stride):
    count = lax.axis_size(axis)
    route = []
    for low in range(count):
        high = low | 1 << stride
        if high != low and high < count:
            route += [(low, high), (high, low)]
    return lax.ppermute(block, axis, route)


def local_partner(values, distance):
    count, blocks, width = values.shape
    folded = values.reshape(count, blocks // (2 * distance), 2, distance, width)
    return folded[:, :, ::-1].reshape(count, blocks, width)


def level_of(distance, blocks):
    return (distance // blocks).bit_length() - 1


def forward_partner(values, distance):
    blocks = values.shape[1]
    if distance < blocks:
        return local_partner(values, distance)
    return partner_2(values, "tensor", level_of(distance, blocks))


def backward_partner(values, distance):
    blocks = values.shape[1]
    if distance < blocks:
        return local_partner(values, distance)
    return partner_2(values, "tensor", level_of(distance, blocks))


def again_partner(values, distance):
    blocks = values.shape[1]
    if distance < blocks:
        return local_partner(values, distance)
    return partner_2(values, "tensor", level_of(distance, blocks))


def grad_block(gathered_input, following_gradient, scale_factor):
    return scale_factor * jnp.einsum(
        "urs,urd->srd", gathered_input, following_gradient, preferred_element_type=jnp.float32
    )


def plain_device(tokens, weights, upstream):
    tok_count = tokens.shape[0]
    blocks = tokens.shape[1] // BLOCK_FEATURES
    scale_factor = 1.0 / math.sqrt(tok_count * lax.axis_size("dp"))
    layer_number = tokens.reshape(tok_count, blocks, BLOCK_FEATURES)
    inputs_saved = []
    partners_saved = []
    for factor_matrix in range(FACTORS):
        partner = forward_partner(layer_number, 2**factor_matrix)
        inputs_saved.append(layer_number)
        partners_saved.append(partner)
        gathered_input = jnp.concatenate([layer_number, partner], axis=2)
        layer_number = jnp.einsum(
            "hjk,kjg->hjg",
            gathered_input,
            weights[:, :, factor_matrix, :],
            preferred_element_type=jnp.float32,
        ).astype(jnp.bfloat16)
    last = layer_number.astype(jnp.float32)
    activated = jax.nn.gelu(last).astype(jnp.bfloat16).reshape(tok_count, blocks * BLOCK_FEATURES)
    _, pull = jax.vjp(jax.nn.gelu, last)
    current_gradient = pull(
        upstream.reshape(tok_count, blocks, BLOCK_FEATURES).astype(jnp.float32)
    )[0].astype(jnp.bfloat16)
    joined_all = [None] * FACTORS
    grads_next = [None] * FACTORS
    for factor_matrix in reversed(range(FACTORS)):
        distance = 2**factor_matrix
        factor_weight = weights[:, :, factor_matrix, :]
        partner = again_partner(inputs_saved[factor_matrix], distance)
        gathered_input = jnp.concatenate([inputs_saved[factor_matrix], partner], axis=2)
        joined_all[factor_matrix] = gathered_input
        grads_next[factor_matrix] = current_gradient
        passed_input = jnp.einsum(
            "jvu,rvu->jvr",
            current_gradient,
            factor_weight[BLOCK_FEATURES:],
            preferred_element_type=jnp.float32,
        ).astype(jnp.bfloat16)
        self_portion = jnp.einsum(
            "jvu,rvu->jvr",
            current_gradient,
            factor_weight[:BLOCK_FEATURES],
            preferred_element_type=jnp.float32,
        )
        arrived = backward_partner(passed_input, distance)
        current_gradient = (self_portion + arrived.astype(jnp.float32)).astype(jnp.bfloat16)
    pieces = [
        grad_block(joined_all[factor_matrix], grads_next[factor_matrix], scale_factor)
        for factor_matrix in range(FACTORS)
    ]
    weight_grad = lax.psum_scatter(jnp.stack(pieces, axis=2), "dp", scatter_dimension=0, tiled=True)
    token_grad = current_gradient.reshape(tok_count, blocks * BLOCK_FEATURES)
    return (activated, token_grad, weight_grad)


SKEW = 2
REDO = (3,)
ORDER = (0, 2, 1, 3)
MESH = pl.DeviceIdType.MESH
W = BLOCK_FEATURES
NN = (((1,), (0,)), ((), ()))
NT = (((1,), (1,)), ((), ()))
TN = (((0,), (0,)), ((), ()))
GELU_A = 0.7978845608
GELU_B = 0.044715


def dot(a, b, dims):
    return lax.dot_general(a, b, dims, preferred_element_type=jnp.float32)


def flip(index, bit):
    return index + bit - 2 * bit * (lax.rem(index // bit, 2))


def fused_kernel(
    scale_factor,
    tok_ref,
    up_ref,
    w,
    act_out,
    tg_out,
    wg_out,
    w_far,
    up_far,
    z,
    part,
    grad,
    hand,
    hand_in,
    self_part,
    act,
    tgrad,
    wg,
    wg_core,
    wg_sum,
    wg_in,
    wg_fin,
    out_sem,
    z_send,
    z_recv,
    core_send,
    core_recv,
    chip_send,
    chip_recv,
    far_send,
    far_recv,
    share_send,
    share_recv,
):
    rows = tok_ref.shape[0]
    blocks = tok_ref.shape[1] // W
    shard = wg_fin.shape[2]
    dp = lax.axis_index("dp")
    tensor = lax.axis_index("tensor")
    core = lax.rem(dp, 2)
    chip = dp // 2

    near = (dp, flip(tensor, 1))
    far = (dp, flip(tensor, 2))
    sibling = (flip(dp, 1), tensor)
    chips = [flip(chip, 1), flip(chip, 2), 3 - chip]
    others = [(2 * c + core, tensor) for c in chips]

    barrier = pltpu.get_barrier_semaphore()
    peers = [dp]
    for bit in (1, 2, 4):
        peers += [flip(p, bit) for p in peers]
    for device in [near, far] + [(p, tensor) for p in peers[1:]]:
        pl.semaphore_signal(barrier, inc=1, device_id=device, device_id_type=MESH)
    pl.semaphore_wait(barrier, 9)
    mine = pl.ds(pl.multiple_of(dp * shard, shard), shard)

    def far_copy(r, what):
        i = REDO[r]
        src = up_ref.at[:, i * W : (i + 1) * W] if what else w.at[3, i, mine]
        return pltpu.make_async_remote_copy(
            src_ref=src,
            dst_ref=up_far.at[r] if what else w_far.at[r, mine],
            send_sem=far_send.at[r, what],
            recv_sem=far_recv.at[r, what],
            device_id=far,
            device_id_type=MESH,
        )

    def share_copy(r, m, sender=None):
        rows_of = pl.ds(pl.multiple_of((dp if sender is None else sender) * shard, shard), shard)
        return pltpu.make_async_remote_copy(
            src_ref=w_far.at[r, rows_of],
            dst_ref=w_far.at[r, rows_of],
            send_sem=share_send.at[r, m - 1],
            recv_sem=share_recv.at[r, m - 1],
            device_id=(peers[m], tensor),
            device_id_type=MESH,
        )

    for what in (0, 1):
        for r in range(len(REDO)):
            far_copy(r, what).start()

    def col(i):
        return slice(i * W, (i + 1) * W)

    half_rows = rows // 2

    def half_of(h):
        return slice(h * half_rows, (h + 1) * half_rows)

    def z_copy(stage, i, h):
        src = (z.at[2], z.at[3], hand.at[1], hand.at[0])[stage]
        dst = (part.at[0], part.at[1], hand_in.at[1], hand_in.at[0])[stage]
        return pltpu.make_async_remote_copy(
            src_ref=src.at[i, pl.ds(h * half_rows, half_rows)],
            dst_ref=dst.at[i, pl.ds(h * half_rows, half_rows)],
            send_sem=z_send.at[stage, i, h],
            recv_sem=z_recv.at[stage, i, h],
            device_id=(near, far, far, near)[stage],
            device_id_type=MESH,
        )

    def z_value(k, i, at=slice(None)):
        return tok_ref[at, col(i)] if k == 0 else z[k, i, at]

    def partner_value(k, i, at=slice(None)):
        return z_value(k, i ^ (1 << k), at) if k < 2 else part[k - 2, i, at]

    def factor(k, i, at=slice(None)):
        total = dot(z_value(k, i, at), w[k, i, :W, :], NN)
        return (total + dot(partner_value(k, i, at), w[k, i, W:, :], NN)).astype(jnp.bfloat16)

    def stage_f1(i, h):
        z[2, i, half_of(h)] = factor(1, i, half_of(h))
        z_copy(0, i, h).start()

    def stage_f2(i, h):
        z_copy(0, i, h).wait_recv()
        z[3, i, half_of(h)] = factor(2, i, half_of(h))
        z_copy(1, i, h).start()

    def gelu_slope(v):
        square = v * v
        t = jnp.tanh(GELU_A * (v + GELU_B * (v * square)))
        half = 0.5 * (1.0 + t)
        slope = half + (0.5 * v) * (1.0 - t * t) * (GELU_A * (1.0 + 3.0 * GELU_B * square))
        return half, slope

    def stage_f3(i, h):
        at = half_of(h)
        z_copy(1, i, h).wait_recv()
        v = factor(3, i, at).astype(jnp.float32)
        half, slope = gelu_slope(v)
        act[at, col(i)] = (v * half).astype(jnp.bfloat16)
        g = (up_ref[at, col(i)].astype(jnp.float32) * slope).astype(jnp.bfloat16)
        grad[3, i, at] = g
        if i in REDO:
            r = REDO.index(i)
            if h == 0:
                for m in range(1, len(peers)):
                    share_copy(r, m, peers[m]).wait_recv()
                far_copy(r, 1).wait_recv()
            v = dot(part[1, i, at], w_far[r, :W, :], NN) + dot(z[3, i, at], w_far[r, W:, :], NN)
            _, slope = gelu_slope(v.astype(jnp.bfloat16).astype(jnp.float32))
            g = (up_far[r, at].astype(jnp.float32) * slope).astype(jnp.bfloat16)
            hand_in[1, i, at] = dot(g, w_far[r, W:, :], NT).astype(jnp.bfloat16)
        else:
            hand[1, i, at] = dot(g, w[3, i, W:, :], NT).astype(jnp.bfloat16)
            z_copy(2, i, h).start()
        self_part[1, i, at] = dot(grad[3, i, at], w[3, i, :W, :], NT)
        if i in REDO:
            stage_b3(i, h)
        if h == 1:
            weight_terms(3, i)

    def stage_b3(i, h):
        at = half_of(h)
        if i not in REDO:
            z_copy(2, i, h).wait_recv()
        g = (self_part[1, i, at] + hand_in[1, i, at].astype(jnp.float32)).astype(jnp.bfloat16)
        grad[2, i, at] = g
        hand[0, i, at] = dot(g, w[2, i, W:, :], NT).astype(jnp.bfloat16)
        z_copy(3, i, h).start()
        self_part[0, i, at] = dot(grad[2, i, at], w[2, i, :W, :], NT)
        if h == 1:
            weight_terms(2, i)

    def stage_b2(i, h):
        at = half_of(h)
        z_copy(3, i, h).wait_recv()
        g = self_part[0, i, at] + hand_in[0, i, at].astype(jnp.float32)
        grad[1, i, at] = g.astype(jnp.bfloat16)
        if h == 1:
            weight_terms(1, i)

    def stage_local(k, i, j):
        both = {m: dot(grad[k, m], w[k, m], NT) for m in (i, j)}
        for m, n in ((i, j), (j, i)):
            handed = both[n][:, W:].astype(jnp.bfloat16).astype(jnp.float32)
            g = (both[m][:, :W] + handed).astype(jnp.bfloat16)
            if k == 1:
                grad[0, m] = g
            else:
                tgrad[:, col(m)] = g

    def core_copy(k, i):
        return pltpu.make_async_remote_copy(
            src_ref=wg.at[k, i, 1 - core],
            dst_ref=wg_core.at[k, i],
            send_sem=core_send.at[k, i],
            recv_sem=core_recv.at[k, i],
            device_id=sibling,
            device_id_type=MESH,
        )

    def chip_copy(k, i, m):
        return pltpu.make_async_remote_copy(
            src_ref=wg_sum.at[k, i, chips[m]],
            dst_ref=wg_in.at[k, i, m],
            send_sem=chip_send.at[k, i, m],
            recv_sem=chip_recv.at[k, i, m],
            device_id=others[m],
            device_id_type=MESH,
        )

    def weight_terms(k, i):
        per = W // shard
        g = grad[k, i]
        for side, left in enumerate((z_value(k, i), partner_value(k, i))):
            total = dot(left, g, TN).astype(jnp.bfloat16)
            for j in range(per):
                at = side * per + j
                wg[k, i, at % 2, at // 2] = total[j * shard : (j + 1) * shard]
        core_copy(k, i).start()

    def weight_sum(k, i):
        core_copy(k, i).wait_recv()
        kept = wg[k, i, core].astype(jnp.float32)
        wg_sum[k, i] = (kept + wg_core[k, i].astype(jnp.float32)).astype(jnp.bfloat16)
        for m in (2, 0, 1):
            chip_copy(k, i, m).start()

    def weight_final(k, i):
        total = wg_sum[k, i, chip].astype(jnp.float32)
        for m in range(3):
            chip_copy(k, i, m).wait_recv()
            total = total + wg_in[k, i, m].astype(jnp.float32)
        wg_fin[k, i] = total * scale_factor

    outs = []

    def store(src, dst, slot):
        outs.append(pltpu.make_async_copy(src, dst, out_sem.at[slot]))
        outs[-1].start()

    for i in range(blocks):
        z[1, i] = factor(0, i)

    order = ORDER
    work = []
    for p, (i, h) in enumerate((i, h) for i in order for h in range(2)):
        for stage, run in enumerate((stage_f1, stage_f2, stage_f3, stage_b3, stage_b2)):
            if i in REDO and run is stage_b3:
                continue
            work.append((p + SKEW * stage, -stage, functools.partial(run, i, h)))
        for k, stage in ((3, 2), (2, 3)):
            if h == 1:
                work.append((p + SKEW * stage + 1, 1, functools.partial(weight_sum, k, i)))
    def share():
        for r in range(len(REDO)):
            far_copy(r, 0).wait_recv()
            for m in (6, 7, 2, 3, 4, 5, 1):
                share_copy(r, m).start()

    work.append((1, 1, functools.partial(share)))
    for _, _, run in sorted(work, key=lambda item: item[:2]):
        if run.func is stage_b2 and run.args == (1, 0):
            store(act, act_out, 0)
            stage_local(1, 0, 2)
            weight_terms(0, 0)
            weight_terms(0, 2)
            weight_sum(1, 0)
            weight_sum(1, 2)
        run()
        if run.func is stage_b2 and run.args == (1, 0):
            weight_sum(0, 0)
            weight_sum(0, 2)
    stage_local(1, 1, 3)
    weight_terms(0, 1)
    weight_terms(0, 3)
    for k, i in ((1, 1), (1, 3), (0, 1), (0, 3)):
        weight_sum(k, i)
    stage_local(0, 0, 1)
    stage_local(0, 2, 3)
    store(tgrad, tg_out, 1)
    for k in (3, 2, 1, 0):
        for i in order:
            weight_final(k, i)
        store(wg_fin.at[k], wg_out.at[k], 2 + k)
    for i in range(blocks):
        for stage in range(4):
            if stage != 2 or i not in REDO:
                for h in range(2):
                    z_copy(stage, i, h).wait_send()
        for k in range(FACTORS):
            core_copy(k, i).wait_send()
            for m in range(3):
                chip_copy(k, i, m).wait_send()
    for r in range(len(REDO)):
        for what in (0, 1):
            far_copy(r, what).wait_send()
        for m in range(1, len(peers)):
            share_copy(r, m).wait_send()
    for copy in outs:
        copy.wait()


def finish_kernel(act_ref, tg_ref, wg_ref, act_out, tg_out, wg_out):
    act_out[...] = act_ref[...]
    tg_out[...] = tg_ref[...]
    for k in range(FACTORS):
        for i in range(wg_ref.shape[1]):
            wg_out[:, i, k, :] = wg_ref[k, i]


def fused_device(tokens, weights, upstream):
    rows, width = tokens.shape
    blocks = width // W
    dp = lax.axis_size("dp")
    shard = 2 * W // dp
    scale_factor = 1.0 / math.sqrt(rows * dp)
    w = weights.transpose(2, 1, 0, 3)
    bf16, f32 = jnp.bfloat16, jnp.float32
    dma = pltpu.SemaphoreType.DMA
    whole = pltpu.VMEM((rows, width), bf16)
    activated, token_grad, weight_grad = pl.pallas_call(
        functools.partial(fused_kernel, scale_factor),
        out_shape=(
            jax.ShapeDtypeStruct((rows, width), bf16),
            jax.ShapeDtypeStruct((rows, width), bf16),
            jax.ShapeDtypeStruct((FACTORS, blocks, shard, W), f32),
        ),
        in_specs=[
            pl.BlockSpec(memory_space=pltpu.VMEM),
            pl.BlockSpec(memory_space=pltpu.VMEM),
            pl.BlockSpec(memory_space=pltpu.VMEM),
        ],
        out_specs=[pl.BlockSpec(memory_space=pl.ANY)] * 3,
        scratch_shapes=[
            pltpu.VMEM((len(REDO), 2 * W, W), bf16),
            pltpu.VMEM((len(REDO), rows, W), bf16),
            pltpu.VMEM((4, blocks, rows, W), bf16),
            pltpu.VMEM((2, blocks, rows, W), bf16),
            pltpu.VMEM((4, blocks, rows, W), bf16),
            pltpu.VMEM((2, blocks, rows, W), bf16),
            pltpu.VMEM((2, blocks, rows, W), bf16),
            pltpu.VMEM((2, blocks, rows, W), f32),
            whole,
            whole,
            pltpu.VMEM((FACTORS, blocks, 2, 4, shard, W), bf16),
            pltpu.VMEM((FACTORS, blocks, 4, shard, W), bf16),
            pltpu.VMEM((FACTORS, blocks, 4, shard, W), bf16),
            pltpu.VMEM((FACTORS, blocks, 3, shard, W), bf16),
            pltpu.VMEM((FACTORS, blocks, shard, W), f32),
            dma((2 + FACTORS,)),
            dma((4, blocks, 2)),
            dma((4, blocks, 2)),
            dma((FACTORS, blocks)),
            dma((FACTORS, blocks)),
            dma((FACTORS, blocks, 3)),
            dma((FACTORS, blocks, 3)),
            dma((len(REDO), 2)),
            dma((len(REDO), 2)),
            dma((len(REDO), 7)),
            dma((len(REDO), 7)),
        ],
        compiler_params=pltpu.CompilerParams(
            collective_id=0, has_side_effects=True, vmem_limit_bytes=40 * 1024 * 1024
        ),
        name="butterfly",
    )(tokens, upstream, w)
    return pl.pallas_call(
        finish_kernel,
        out_shape=(
            jax.ShapeDtypeStruct((rows, width), bf16),
            jax.ShapeDtypeStruct((rows, width), bf16),
            jax.ShapeDtypeStruct((shard, blocks, FACTORS, W), f32),
        ),
        in_specs=[pl.BlockSpec(memory_space=pltpu.VMEM)] * 3,
        out_specs=[pl.BlockSpec(memory_space=pltpu.VMEM)] * 3,
        compiler_params=pltpu.CompilerParams(vmem_limit_bytes=16 * 1024 * 1024),
        name="finish",
    )(activated, token_grad, weight_grad)


def on_device(tokens, weights, upstream):
    blocks = tokens.shape[1] // BLOCK_FEATURES
    fits = (
        lax.axis_size("dp") == 8
        and lax.axis_size("tensor") == 4
        and blocks == 4
        and tokens.shape[0] % 32 == 0
        and tokens.shape[0] <= 256
    )
    if fits:
        return fused_device(tokens, weights, upstream)
    return plain_device(tokens, weights, upstream)


def solution(mesh):
    placed = (P("dp", "tensor"), P(None, "tensor", None, None), P("dp", "tensor"))
    return jax.shard_map(
        on_device,
        mesh=mesh,
        in_specs=placed,
        out_specs=(P("dp", "tensor"), P("dp", "tensor"), P("dp", "tensor", None, None)),
        check_vma=False,
    )
```
